32 devices in a mesh: grp: 4 (over x, core), exc: 2 (over y), col: 4 (over z).
Axes of the slice: x: 2, y: 2, z: 4, core: 2. Of those that a mesh axis runs over, the one named last changes fastest.
Arguments:
- window_factor: float32 [1024, 8, 512], P('exc', 'grp'), may hold values from -0.375 to 0.375
- fitted_factor: float32 [1024, 512, 512], P('exc', 'col'), may hold values from -0.375 to 0.375
- pair_amps: float32 [16, 512, 512], P(None, 'col'), may hold values from -0.1875 to 0.1875
- cycle_amps: float32 [16, 32768], P(None, ('grp', 'exc')), may hold values from -6 to 6
- panel: float32 [32768, 4096], P(('grp', 'exc'), 'col'), may hold values from -0.03125 to 0.03125
Outputs:
- sigma: float32 [16, 4096], P(('grp', 'exc'), 'col')
The draws below stay inside these ranges and needn't reach their ends.
All inputs are finite; a program needn't handle non-finite values.
Results may differ from the reference program's by a relative error of at most 0.0001.
Values sent between devices are 32-bit elements; how exact they have to be, the bound alone decides.
No kernel may reach another device: no remote copies, remote signals or barrier semaphores. Data moves between devices by JAX's collectives and lax.ppermute only.
A program may use at most 256 MiB of HBM per device.

```python
import math
import jax
import jax.numpy as jnp
from jax import lax

V = 512
NAUX = 1024
NI = 2
NJ = 8
NA = 8
ROWS = 16
NPAIR = 16
KDIM = 32768
NCOL = 4096


def strengthened(entries, own_key, source, target, parts, factor):
    def block_of(dim):
        return (jnp.arange(entries.shape[dim]) // (entries.shape[dim] // parts)).reshape((-1,) + (1,) * (entries.ndim - 1 - dim))

    first = jax.random.permutation(own_key, parts)[block_of(target)]
    second = (block_of(target) + parts // 2) % parts
    return jnp.where((block_of(source) == first) | (block_of(source) == second), factor * entries, entries)


def block_scale(own_key, shape, cuts, smallest, high):
    loudness, own = 1.0, jax.random.fold_in(own_key, 6)
    for dim, shards_of in cuts:
        heights = jnp.exp(jax.random.uniform(jax.random.fold_in(own, dim), (shards_of,), jnp.float32, smallest / len(cuts), high / len(cuts)))
        loudness = loudness * jnp.repeat(heights, shape[dim] // shards_of).reshape([-1 if axis == dim else 1 for axis in range(len(shape))])
    return loudness


def scatter_about(stream_key, extent, deviation, most, split=(), dtype=jnp.bfloat16):
    factor_of = block_scale(stream_key, extent, split, -0.22, 0.18) if split else 1.0
    values = jax.random.normal(stream_key, extent, jnp.float32) * deviation * factor_of
    return jnp.minimum(jnp.maximum(values, -most), most).astype(dtype)


def gaussian_with(own_key, dims, scale, most, shards, heavy, held_as=jnp.bfloat16):
    array = scale * jax.random.normal(own_key, dims, jnp.float32)
    if shards:
        array = array * block_scale(own_key, dims, shards, -0.22, 0.18)
    return jnp.clip(strengthened(array, jax.random.fold_in(own_key, 3), *heavy), -most, most).astype(held_as)


def setup_inputs(seed: int = 0) -> dict:
    key_list = jax.random.split(jax.random.key(seed), 6)
    return {
        "window_factor": gaussian_with(key_list[0], (NAUX, NA, V), V ** -0.5, 0.375, ((0, 2), (1, 4)), (0, 1, 4, 2.0), jnp.float32),
        "fitted_factor": gaussian_with(key_list[1], (NAUX, V, V), V ** -0.5, 0.375, ((0, 2), (1, 4)), (1, 2, 4, 2.0), jnp.float32),
        "pair_amps": scatter_about(key_list[2], (NPAIR, V, V), NAUX ** -0.5, 0.1875, ((1, 4),), jnp.float32),
        "cycle_amps": gaussian_with(key_list[3], (ROWS, KDIM), 1.0, 6.0, ((1, 8),), (1, 0, 8, 2.0), jnp.float32),
        "panel": scatter_about(key_list[4], (KDIM, NCOL), KDIM ** -0.5, 0.03125, ((0, 8), (1, 4)), jnp.float32),
    }


def reference(window_factor, fitted_factor, pair_amps, cycle_amps, panel):
    precise = lax.Precision.HIGHEST
    block = math.gcd(NAUX, 64)
    count = NAUX // block
    amplitude = pair_amps.reshape(NI, NJ, V, V)
    windows = window_factor.reshape(count, block, NA, V)
    fitted = fitted_factor.reshape(count, block, V, V)

    def accumulate(total, pieces):
        window_part, fitted_part = pieces
        inner = jnp.einsum('pac,ijdc->aijpd', window_part, amplitude, precision=precise)
        added = jnp.einsum('aijpd,pdb->aijb', inner, fitted_part, precision=precise)
        return total + added, None

    start = jnp.zeros((NA, NI, NJ, V), jnp.float32)
    total, _ = lax.scan(accumulate, start, (windows, fitted))
    ladder = total.reshape(NA * NI, NJ * V)
    cycle = jnp.dot(cycle_amps, panel, precision=precise, preferred_element_type=jnp.float32)
    return ladder + cycle
```

```python
import functools

import jax
import jax.numpy as jnp
from jax import lax
from jax.experimental import pallas as pl
from jax.experimental.pallas import tpu as pltpu
from jax.sharding import PartitionSpec as P

NI = 2
NJ = 8
VMEM_BYTES = 56 * 1024 * 1024
LANES = 128


def split(x):
    high = x.astype(jnp.bfloat16)
    low = (x - high.astype(jnp.float32)).astype(jnp.bfloat16)
    return high, low


def dot(x, y):
    return jnp.dot(x, y, preferred_element_type=jnp.float32)


def dot_t(x, y):
    return lax.dot_general(x, y, (((1,), (1,)), ((), ())), preferred_element_type=jnp.float32)


def plain(window_factor, fitted_factor, pair_amps, cycle_amps, panel):
    precise = lax.Precision.HIGHEST
    aux_count, virt_count, virtuals = window_factor.shape
    fit_count = fitted_factor.shape[1]
    amplitude = pair_amps.reshape(NI, NJ, fit_count, virtuals)
    inner = jnp.einsum("pac,ijdc->aijpd", window_factor, amplitude, precision=precise)
    inner_rows = inner.reshape(virt_count * NI * NJ, aux_count * fit_count)
    fitted_rows = fitted_factor.reshape(aux_count * fit_count, virtuals)
    ladder_terms = jnp.dot(inner_rows, fitted_rows, precision=precise, preferred_element_type=jnp.float32)
    ladder_terms = ladder_terms.reshape(virt_count * NI, NJ * virtuals)
    cycle_part = jnp.dot(cycle_amps, panel, precision=precise, preferred_element_type=jnp.float32)
    partial_value = lax.psum_scatter(ladder_terms, "col", scatter_dimension=1, tiled=True)
    ladder = lax.psum_scatter(partial_value, "exc", scatter_dimension=0, tiled=True)
    cycle = lax.psum_scatter(cycle_part, ("grp", "exc"), scatter_dimension=0, tiled=True)
    return ladder + cycle


def cycle_kernel(place, amps_ref, panel_ref, out_ref, total):
    step = pl.program_id(0)

    @pl.when(step == 0)
    def _():
        total[...] = jnp.zeros_like(total)

    high, low = split(amps_ref[...])
    panel_high, panel_low = split(panel_ref[...])
    rows = high.shape[0]
    both = dot(jnp.concatenate([high, low], axis=0), panel_high)
    total[...] += both[:rows] + both[rows:] + dot(high, panel_low)

    @pl.when(step == pl.num_programs(0) - 1)
    def _():
        for slot in range(rows // NI):
            row = (place[0] ^ slot) * NI
            for i in range(NI):
                out_ref[slot, pl.ds(i, 1), :] = total[pl.ds(row + i, 1), :]


def cycle_slots(place, cycle_amps, panel):
    rows, depth = cycle_amps.shape
    columns = panel.shape[1]
    block = min(512, depth)
    return pl.pallas_call(
        cycle_kernel,
        out_shape=jax.ShapeDtypeStruct((rows // NI, NI, columns), jnp.float32),
        grid_spec=pltpu.PrefetchScalarGridSpec(
            num_scalar_prefetch=1,
            grid=(depth // block,),
            in_specs=[
                pl.BlockSpec((rows, block), lambda s, place: (0, s)),
                pl.BlockSpec((block, columns), lambda s, place: (s, 0)),
            ],
            out_specs=pl.BlockSpec((rows // NI, NI, columns), lambda s, place: (0, 0, 0)),
            scratch_shapes=[pltpu.VMEM((rows, columns), jnp.float32)],
        ),
        compiler_params=pltpu.CompilerParams(vmem_limit_bytes=VMEM_BYTES),
        cost_estimate=pl.CostEstimate(
            flops=6 * rows * depth * columns, bytes_accessed=4 * depth * columns, transcendentals=0
        ),
    )(place, cycle_amps, panel)


DEPTH = 16
GROUP = 4


def ladder_kernel(place, own_ref, other_ref, amp_ref, fitted_ref, keep_ref, send_ref,
                  amp_high, amp_low, rows_ref, left, total):
    step = pl.program_id(0)
    steps = pl.num_programs(0)
    pairs, fit_count, virtuals = amp_ref.shape
    a_count = own_ref.shape[1]
    core, exc, col = place[1], place[2], place[3]
    half = 2 * a_count * pairs // 2
    m = 2 * a_count * pairs

    @pl.when(step == 0)
    def _():
        total[...] = jnp.zeros_like(total)
        for pair in range(pairs):
            high, low = split(amp_ref[pair])
            amp_high[pl.ds(pair * fit_count, fit_count), :] = high
            amp_low[pl.ds(pair * fit_count, fit_count), :] = low

    @pl.when(step % GROUP == 0)
    def _():
        count = DEPTH * GROUP
        first = (core * steps + step) * DEPTH
        for p in range(count):
            rows_ref[pl.ds(2 * a_count * p, a_count), :] = own_ref[first + p]
            rows_ref[pl.ds(2 * a_count * p + a_count, a_count), :] = other_ref[first + p]
        high, low = split(rows_ref[...])
        stacked = jnp.concatenate([high, low], axis=0)
        n_rows = high.shape[0]
        upper = lax.broadcasted_iota(jnp.int32, (n_rows // 8, 8, LANES), 1) < 4

        for quad in range(pairs // 4):
            lanes = pl.ds(quad * 4 * fit_count, 4 * fit_count)
            weights = amp_high[lanes, :]
            both = dot_t(stacked, weights)
            product = both[:n_rows] + both[n_rows:] + dot_t(high, amp_low[lanes, :])
            for odd in range(2):
                tiles = []
                for duo in range(2):
                    one = product[:, (2 * duo) * LANES : (2 * duo + 1) * LANES].reshape(n_rows // 8, 8, LANES)
                    two = product[:, (2 * duo + 1) * LANES : (2 * duo + 2) * LANES].reshape(n_rows // 8, 8, LANES)
                    if odd:
                        tiles.append(jnp.where(upper, pltpu.roll(one, 4, 1), two))
                    else:
                        tiles.append(jnp.where(upper, one, pltpu.roll(two, 4, 1)))
                tile_high, tile_low = split(jnp.concatenate(tiles, axis=1))
                for index in range(n_rows // 8):
                    slot, place_in = divmod(2 * index + odd, DEPTH)
                    left[slot, pl.ds(16 * quad, 16), pl.ds(place_in * LANES, LANES)] = tile_high[index]
                    left[slot, pl.ds(m + 16 * quad, 16), pl.ds(place_in * LANES, LANES)] = tile_low[index]

    slot = step % GROUP
    part = 4
    for piece in range(DEPTH // part):
        fitted = fitted_ref[pl.ds(piece * part, part)].reshape(part * fit_count, virtuals)
        fitted_high, fitted_low = split(fitted)
        lanes = pl.ds(piece * part * LANES, part * LANES)
        both = dot(left[slot, :, lanes], fitted_high)
        total[...] += both[:m] + both[m:] + dot(left[slot, pl.ds(0, m), lanes], fitted_low)

    @pl.when(step == steps - 1)
    def _():
        cols = NJ // 2
        for target, out in ((0, keep_ref), (1, send_ref)):
            for far in range(2):
                for away in range(cols):
                    for i in range(NI):
                        for j in range(2):
                            pair = i * NJ + (col ^ away) * 2 + j
                            row = pair * 2 * a_count + target * a_count + (exc ^ far)
                            out[far, pl.ds(away * NI + i, 1), pl.ds(j * virtuals, virtuals)] = total[pl.ds(row, 1), :]


def ladder_slots(place, own, other, pair_amps, fitted_factor):
    pairs, fit_count, virtuals = pair_amps.shape
    aux_count, a_count = own.shape[:2]
    steps = aux_count // 2 // DEPTH
    m = 2 * a_count * pairs
    whole = lambda *shape: pl.BlockSpec(shape, lambda s, place: (0,) * len(shape), pipeline_mode=pl.Buffered(1))
    out = jax.ShapeDtypeStruct((2, NJ, 2 * virtuals), jnp.float32)
    out_spec = pl.BlockSpec(out.shape, lambda s, place: (0, 0, 0))
    return pl.pallas_call(
        ladder_kernel,
        out_shape=(out, out),
        grid_spec=pltpu.PrefetchScalarGridSpec(
            num_scalar_prefetch=1,
            grid=(steps,),
            in_specs=[
                whole(*own.shape),
                whole(*own.shape),
                whole(*pair_amps.shape),
                pl.BlockSpec((DEPTH, fit_count, virtuals), lambda s, place: (place[1] * steps + s, 0, 0)),
            ],
            out_specs=(out_spec, out_spec),
            scratch_shapes=[
                pltpu.VMEM((pairs * fit_count, virtuals), jnp.bfloat16),
                pltpu.VMEM((pairs * fit_count, virtuals), jnp.bfloat16),
                pltpu.VMEM((DEPTH * GROUP * 2 * a_count, virtuals), jnp.float32),
                pltpu.VMEM((GROUP, 2 * m, DEPTH * LANES), jnp.bfloat16),
                pltpu.VMEM((m, virtuals), jnp.float32),
            ],
        ),
        compiler_params=pltpu.CompilerParams(vmem_limit_bytes=VMEM_BYTES),
        cost_estimate=pl.CostEstimate(
            flops=6 * aux_count * a_count * pairs * fit_count * virtuals * 2,
            bytes_accessed=2 * aux_count * fit_count * virtuals, transcendentals=0
        ),
    )(place, own, other, pair_amps, fitted_factor)


def swap(x, axis, size, bit):
    return lax.ppermute(x, axis, [(n, n ^ bit) for n in range(size)])


def fast(grp_count, exc_count, col_count, window_factor, fitted_factor, pair_amps, cycle_amps, panel):
    grp, exc, col = lax.axis_index("grp"), lax.axis_index("exc"), lax.axis_index("col")
    place = jnp.stack([grp * exc_count + exc, grp % 2, exc, col]).astype(jnp.int32)
    other = swap(window_factor, "grp", grp_count, 1)
    cycle = cycle_slots(place, cycle_amps, panel)
    cycle_far = swap(cycle[4:], "grp", grp_count, 2)
    keep, send = ladder_slots(place, window_factor, other, pair_amps, fitted_factor)
    near = cycle[:4] + cycle_far
    near = near.reshape(2, 2, NI, -1)
    send = send.at[:, :NI].add(near[1])
    keep = keep.at[:, :NI].add(near[0])
    total = keep + swap(send, "grp", grp_count, 1)
    total = total[0] + swap(total[1], "exc", exc_count, 1)
    bit = col_count // 2
    while bit:
        total = total[: bit * NI] + swap(total[bit * NI :], "col", col_count, bit)
        bit //= 2
    return total


def solution(mesh):
    placed = (
        P("exc", "grp", None),
        P("exc", "col", None),
        P(None, "col", None),
        P(None, ("grp", "exc")),
        P(("grp", "exc"), "col"),
    )
    grp_count, exc_count, col_count = (mesh.shape[name] for name in ("grp", "exc", "col"))

    def shards(window_factor, fitted_factor, pair_amps, cycle_amps, panel):
        aux_count, a_count, virtuals = window_factor.shape
        fits = (
            grp_count == 4
            and exc_count == 2
            and a_count == 2
            and 2 * col_count == NJ
            and fitted_factor.shape[1] == LANES
            and virtuals % LANES == 0
            and aux_count % (2 * DEPTH * GROUP) == 0
        )
        body = functools.partial(fast, grp_count, exc_count, col_count) if fits else plain
        return body(window_factor, fitted_factor, pair_amps, cycle_amps, panel)

    return jax.shard_map(
        shards, mesh=mesh, in_specs=placed, out_specs=P(("grp", "exc"), "col"), check_vma=False
    )
```

```python
import functools

import jax
import jax.numpy as jnp
from jax import lax
from jax.experimental import pallas as pl
from jax.experimental.pallas import tpu as pltpu
from jax.sharding import PartitionSpec as P

NI = 2
NJ = 8
VMEM_BYTES = 56 * 1024 * 1024
LANES = 128


def split(x):
    high = x.astype(jnp.bfloat16)
    low = (x - high.astype(jnp.float32)).astype(jnp.bfloat16)
    return high, low


def dot(x, y):
    return jnp.dot(x, y, preferred_element_type=jnp.float32)


def dot_t(x, y):
    return lax.dot_general(x, y, (((1,), (1,)), ((), ())), preferred_element_type=jnp.float32)


def plain(window_factor, fitted_factor, pair_amps, cycle_amps, panel):
    precise = lax.Precision.HIGHEST
    aux_count, virt_count, virtuals = window_factor.shape
    fit_count = fitted_factor.shape[1]
    amplitude = pair_amps.reshape(NI, NJ, fit_count, virtuals)
    inner = jnp.einsum("pac,ijdc->aijpd", window_factor, amplitude, precision=precise)
    inner_rows = inner.reshape(virt_count * NI * NJ, aux_count * fit_count)
    fitted_rows = fitted_factor.reshape(aux_count * fit_count, virtuals)
    ladder_terms = jnp.dot(inner_rows, fitted_rows, precision=precise, preferred_element_type=jnp.float32)
    ladder_terms = ladder_terms.reshape(virt_count * NI, NJ * virtuals)
    cycle_part = jnp.dot(cycle_amps, panel, precision=precise, preferred_element_type=jnp.float32)
    partial_value = lax.psum_scatter(ladder_terms, "col", scatter_dimension=1, tiled=True)
    ladder = lax.psum_scatter(partial_value, "exc", scatter_dimension=0, tiled=True)
    cycle = lax.psum_scatter(cycle_part, ("grp", "exc"), scatter_dimension=0, tiled=True)
    return ladder + cycle


STRIP = 512
STRIPS = 3


def cycle_kernel(amps_hbm, panel_ref, near_ref, far_ref, across_ref, amps_ref, strips, total, sems, amps_sem):
    rows, depth = amps_ref.shape
    count = depth // STRIP
    me = lax.axis_index("grp") * lax.axis_size("exc") + lax.axis_index("exc")
    amps_copy = pltpu.make_async_copy(amps_hbm, amps_ref, amps_sem)
    amps_copy.start()

    def fetch(n):
        return pltpu.make_async_copy(panel_ref.at[pl.ds(n * STRIP, STRIP)], strips.at[n], sems.at[n])

    for n in range(min(STRIPS, count)):
        fetch(n).start()
    total[...] = jnp.zeros_like(total)
    amps_copy.wait()
    for n in range(count):
        fetch(n).wait()
        if n + STRIPS < count:
            fetch(n + STRIPS).start()
        high, low = split(amps_ref[:, n * STRIP : (n + 1) * STRIP])
        panel_high, panel_low = split(strips[n])
        both = dot(jnp.concatenate([high, low], axis=0), panel_high)
        total[...] += both[:rows] + both[rows:] + dot(high, panel_low)
    exc_count = lax.axis_size("exc")
    outs = [(near_ref, n) for n in range(2 * exc_count)]
    outs += [(ref, n) for ref in (far_ref, across_ref) for n in range(exc_count)]
    for slot, (out, n) in enumerate(outs):
        row = (me ^ slot) * NI
        for i in range(NI):
            out[n, pl.ds(i, 1), :] = total[pl.ds(row + i, 1), :]


def cycle_slots(cycle_amps, panel):
    rows, depth = cycle_amps.shape
    columns = panel.shape[1]
    near = jax.ShapeDtypeStruct((rows // NI // 2, NI, columns), jnp.float32)
    far = jax.ShapeDtypeStruct((rows // NI // 4, NI, columns), jnp.float32)
    return pl.pallas_call(
        cycle_kernel,
        out_shape=(near, far, far),
        in_specs=[pl.BlockSpec(memory_space=pltpu.HBM)] * 2,
        out_specs=(pl.BlockSpec(memory_space=pltpu.VMEM),) * 3,
        scratch_shapes=[
            pltpu.VMEM((rows, depth), jnp.float32),
            pltpu.VMEM((depth // STRIP, STRIP, columns), jnp.float32),
            pltpu.VMEM((rows, columns), jnp.float32),
            pltpu.SemaphoreType.DMA((depth // STRIP,)),
            pltpu.SemaphoreType.DMA,
        ],
        compiler_params=pltpu.CompilerParams(vmem_limit_bytes=VMEM_BYTES),
        cost_estimate=pl.CostEstimate(
            flops=6 * rows * depth * columns, bytes_accessed=4 * depth * columns, transcendentals=0
        ),
    )(cycle_amps, panel)


DEPTH = 16
GROUP = 4
SLOTS = 6
PART = 2


def ladder_kernel(own_hbm, other_hbm, amp_hbm, fitted_hbm, near_ref, keep_ref, send_ref,
                  own, other, amp, amp_high, amp_low, rows_ref, left, fitted_in, total, sems, fitted_sems):
    pairs, fit_count, virtuals = amp_hbm.shape
    aux_half, a_count = own.shape[:2]
    steps = aux_half // DEPTH
    core, exc, col = lax.axis_index("grp") % 2, lax.axis_index("exc"), lax.axis_index("col")
    first = core * aux_half
    m = 2 * a_count * pairs

    def fetch(step, slot):
        source = fitted_hbm.at[pl.ds(first + step * DEPTH, DEPTH)]
        return pltpu.make_async_copy(source, fitted_in.at[slot], fitted_sems.at[slot])

    small = [
        pltpu.make_async_copy(amp_hbm, amp, sems.at[0]),
        pltpu.make_async_copy(own_hbm.at[pl.ds(first, aux_half)], own, sems.at[1]),
        pltpu.make_async_copy(other_hbm.at[pl.ds(first, aux_half)], other, sems.at[2]),
    ]
    for copy in small:
        copy.start()
    fetch(0, 0).start()
    total[...] = jnp.zeros_like(total)
    small[0].wait()
    fetch(1, 1).start()
    for pair in range(pairs):
        high, low = split(amp[pair])
        amp_high[pl.ds(pair * fit_count, fit_count), :] = high
        amp_low[pl.ds(pair * fit_count, fit_count), :] = low
    small[1].wait()
    small[2].wait()
    for step in range(2, SLOTS):
        fetch(step, step).start()

    def first_product(group):
        count = DEPTH * GROUP
        for p in range(count):
            rows_ref[pl.ds(2 * a_count * p, a_count), :] = own[group * count + p]
            rows_ref[pl.ds(2 * a_count * p + a_count, a_count), :] = other[group * count + p]
        high, low = split(rows_ref[...])
        stacked = jnp.concatenate([high, low], axis=0)
        n_rows = high.shape[0]
        upper = lax.broadcasted_iota(jnp.int32, (n_rows // 8, 8, LANES), 1) < 4

        for quad in range(pairs // 4):
            lanes = pl.ds(quad * 4 * fit_count, 4 * fit_count)
            both = dot_t(stacked, amp_high[lanes, :])
            product = both[:n_rows] + both[n_rows:] + dot_t(high, amp_low[lanes, :])
            for odd in range(2):
                tiles = []
                for duo in range(2):
                    one = product[:, (2 * duo) * LANES : (2 * duo + 1) * LANES].reshape(n_rows // 8, 8, LANES)
                    two = product[:, (2 * duo + 1) * LANES : (2 * duo + 2) * LANES].reshape(n_rows // 8, 8, LANES)
                    if odd:
                        tiles.append(jnp.where(upper, pltpu.roll(one, 4, 1), two))
                    else:
                        tiles.append(jnp.where(upper, one, pltpu.roll(two, 4, 1)))
                tile_high, tile_low = split(jnp.concatenate(tiles, axis=1))
                for index in range(n_rows // 8):
                    slot, place_in = divmod(2 * index + odd, DEPTH)
                    left[slot, pl.ds(16 * quad, 16), pl.ds(place_in * LANES, LANES)] = tile_high[index]
                    left[slot, pl.ds(m + 16 * quad, 16), pl.ds(place_in * LANES, LANES)] = tile_low[index]

    @pl.loop(0, steps // GROUP)
    def _(group):
        first_product(group)
        for near in range(GROUP):
            step = group * GROUP + near
            slot = lax.rem(step, SLOTS)
            fetch(step, slot).wait()
            for piece in range(DEPTH // PART):
                fitted = fitted_in[slot, pl.ds(piece * PART, PART)].reshape(PART * fit_count, virtuals)
                fitted_high, fitted_low = split(fitted)
                lanes = pl.ds(piece * PART * LANES, PART * LANES)
                both = dot(left[near, :, lanes], fitted_high)
                total[...] += both[:m] + both[m:] + dot(left[near, pl.ds(0, m), lanes], fitted_low)

            @pl.when(step + SLOTS < steps)
            def _():
                fetch(step + SLOTS, slot).start()

    for target, out in ((0, keep_ref), (1, send_ref)):
        for far in range(2):
            for away in range(NJ // 2):
                for i in range(NI):
                    for j in range(2):
                        pair = i * NJ + (col ^ away) * 2 + j
                        row = pair * 2 * a_count + target * a_count + (exc ^ far)
                        columns = pl.ds(j * virtuals, virtuals)
                        value = total[pl.ds(row, 1), :]
                        if away == 0:
                            value += near_ref[target * 2 + far, pl.ds(i, 1), columns]
                        out[far, pl.ds(away * NI + i, 1), columns] = value


def ladder_slots(own, other, pair_amps, fitted_factor, near):
    pairs, fit_count, virtuals = pair_amps.shape
    aux_count, a_count = own.shape[:2]
    m = 2 * a_count * pairs
    out = jax.ShapeDtypeStruct((2, NJ, 2 * virtuals), jnp.float32)
    half = (aux_count // 2, a_count, virtuals)
    return pl.pallas_call(
        ladder_kernel,
        out_shape=(out, out),
        in_specs=[
            pl.BlockSpec(memory_space=pltpu.HBM),
            pl.BlockSpec(memory_space=pl.ANY),
            pl.BlockSpec(memory_space=pltpu.HBM),
            pl.BlockSpec(memory_space=pltpu.HBM),
            pl.BlockSpec(memory_space=pltpu.VMEM),
        ],
        out_specs=(pl.BlockSpec(memory_space=pltpu.VMEM),) * 2,
        scratch_shapes=[
            pltpu.VMEM(half, jnp.float32),
            pltpu.VMEM(half, jnp.float32),
            pltpu.VMEM(pair_amps.shape, jnp.float32),
            pltpu.VMEM((pairs * fit_count, virtuals), jnp.bfloat16),
            pltpu.VMEM((pairs * fit_count, virtuals), jnp.bfloat16),
            pltpu.VMEM((DEPTH * GROUP * 2 * a_count, virtuals), jnp.float32),
            pltpu.VMEM((GROUP, 2 * m, DEPTH * LANES), jnp.bfloat16),
            pltpu.VMEM((SLOTS, DEPTH, fit_count, virtuals), jnp.float32),
            pltpu.VMEM((m, virtuals), jnp.float32),
            pltpu.SemaphoreType.DMA((3,)),
            pltpu.SemaphoreType.DMA((SLOTS,)),
        ],
        compiler_params=pltpu.CompilerParams(vmem_limit_bytes=VMEM_BYTES),
        cost_estimate=pl.CostEstimate(
            flops=6 * aux_count * a_count * pairs * fit_count * virtuals * 2,
            bytes_accessed=2 * aux_count * fit_count * virtuals, transcendentals=0
        ),
    )(own, other, pair_amps, fitted_factor, near)


def swap(x, axis, size, bit):
    return lax.ppermute(x, axis, [(n, n ^ bit) for n in range(size)])


def fast(grp_count, exc_count, col_count, window_factor, fitted_factor, pair_amps, cycle_amps, panel):
    other = swap(window_factor, "grp", grp_count, 1)
    near, far, across = cycle_slots(cycle_amps, panel)
    one, two = swap(far, "grp", grp_count, 2), swap(across, "grp", grp_count, 3)
    keep, send = ladder_slots(window_factor, other, pair_amps, fitted_factor, near)
    keep, send, one, two = lax.optimization_barrier((keep, send, one, two))
    total = (keep + swap(send, "grp", grp_count, 1)).at[:, :NI].add(one + two)
    total = total[0] + swap(total[1], "exc", exc_count, 1)
    bit = col_count // 2
    while bit:
        total = total[: bit * NI] + swap(total[bit * NI :], "col", col_count, bit)
        bit //= 2
    return total


def solution(mesh):
    placed = (
        P("exc", "grp", None),
        P("exc", "col", None),
        P(None, "col", None),
        P(None, ("grp", "exc")),
        P(("grp", "exc"), "col"),
    )
    grp_count, exc_count, col_count = (mesh.shape[name] for name in ("grp", "exc", "col"))

    def shards(window_factor, fitted_factor, pair_amps, cycle_amps, panel):
        aux_count, a_count, virtuals = window_factor.shape
        fits = (
            grp_count == 4
            and exc_count == 2
            and a_count == 2
            and 2 * col_count == NJ
            and fitted_factor.shape[1] == LANES
            and virtuals % LANES == 0
            and aux_count % (2 * DEPTH * GROUP) == 0
            and cycle_amps.shape[1] % STRIP == 0
        )
        body = functools.partial(fast, grp_count, exc_count, col_count) if fits else plain
        return body(window_factor, fitted_factor, pair_amps, cycle_amps, panel)

    return jax.shard_map(
        shards, mesh=mesh, in_specs=placed, out_specs=P(("grp", "exc"), "col"), check_vma=False
    )
```

```python
import functools

import jax
import jax.numpy as jnp
from jax import lax
from jax.experimental import pallas as pl
from jax.experimental.pallas import tpu as pltpu
from jax.sharding import PartitionSpec as P

NI = 2
NJ = 8
VMEM_BYTES = 48 * 1024 * 1024
LANES = 128


def split(x):
    high = x.astype(jnp.bfloat16)
    low = (x - high.astype(jnp.float32)).astype(jnp.bfloat16)
    return high, low


def dot(x, y):
    return jnp.dot(x, y, preferred_element_type=jnp.float32)


def dot_t(x, y):
    return lax.dot_general(x, y, (((1,), (1,)), ((), ())), preferred_element_type=jnp.float32)


def plain(window_factor, fitted_factor, pair_amps, cycle_amps, panel):
    precise = lax.Precision.HIGHEST
    aux_count, virt_count, virtuals = window_factor.shape
    fit_count = fitted_factor.shape[1]
    amplitude = pair_amps.reshape(NI, NJ, fit_count, virtuals)
    inner = jnp.einsum("pac,ijdc->aijpd", window_factor, amplitude, precision=precise)
    inner_rows = inner.reshape(virt_count * NI * NJ, aux_count * fit_count)
    fitted_rows = fitted_factor.reshape(aux_count * fit_count, virtuals)
    ladder_terms = jnp.dot(inner_rows, fitted_rows, precision=precise, preferred_element_type=jnp.float32)
    ladder_terms = ladder_terms.reshape(virt_count * NI, NJ * virtuals)
    cycle_part = jnp.dot(cycle_amps, panel, precision=precise, preferred_element_type=jnp.float32)
    partial_value = lax.psum_scatter(ladder_terms, "col", scatter_dimension=1, tiled=True)
    ladder = lax.psum_scatter(partial_value, "exc", scatter_dimension=0, tiled=True)
    cycle = lax.psum_scatter(cycle_part, ("grp", "exc"), scatter_dimension=0, tiled=True)
    return ladder + cycle


STRIP = 512
STRIPS = 3


def cycle_kernel(amps_hbm, panel_ref, near_ref, far_ref, across_ref, amps_ref, strips, total, sems, amps_sem):
    rows, depth = amps_ref.shape
    count = depth // STRIP
    me = lax.axis_index("grp") * lax.axis_size("exc") + lax.axis_index("exc")
    amps_copy = pltpu.make_async_copy(amps_hbm, amps_ref, amps_sem)
    amps_copy.start()

    def fetch(n):
        return pltpu.make_async_copy(panel_ref.at[pl.ds(n * STRIP, STRIP)], strips.at[n], sems.at[n])

    for n in range(min(STRIPS, count)):
        fetch(n).start()
    total[...] = jnp.zeros_like(total)
    amps_copy.wait()
    for n in range(count):
        fetch(n).wait()
        if n + STRIPS < count:
            fetch(n + STRIPS).start()
        high, low = split(amps_ref[:, n * STRIP : (n + 1) * STRIP])
        panel_high, panel_low = split(strips[n])
        both = dot(jnp.concatenate([high, low], axis=0), panel_high)
        total[...] += both[:rows] + both[rows:] + dot(high, panel_low)
    exc_count = lax.axis_size("exc")
    outs = [(near_ref, n) for n in range(2 * exc_count)]
    outs += [(ref, n) for ref in (far_ref, across_ref) for n in range(exc_count)]
    for slot, (out, n) in enumerate(outs):
        row = (me ^ slot) * NI
        for i in range(NI):
            out[n, pl.ds(i, 1), :] = total[pl.ds(row + i, 1), :]


def cycle_slots(cycle_amps, panel):
    rows, depth = cycle_amps.shape
    columns = panel.shape[1]
    near = jax.ShapeDtypeStruct((rows // NI // 2, NI, columns), jnp.float32)
    far = jax.ShapeDtypeStruct((rows // NI // 4, NI, columns), jnp.float32)
    return pl.pallas_call(
        cycle_kernel,
        out_shape=(near, far, far),
        in_specs=[pl.BlockSpec(memory_space=pltpu.HBM)] * 2,
        out_specs=(pl.BlockSpec(memory_space=pltpu.VMEM),) * 3,
        scratch_shapes=[
            pltpu.VMEM((rows, depth), jnp.float32),
            pltpu.VMEM((depth // STRIP, STRIP, columns), jnp.float32),
            pltpu.VMEM((rows, columns), jnp.float32),
            pltpu.SemaphoreType.DMA((depth // STRIP,)),
            pltpu.SemaphoreType.DMA,
        ],
        compiler_params=pltpu.CompilerParams(vmem_limit_bytes=VMEM_BYTES),
        cost_estimate=pl.CostEstimate(
            flops=6 * rows * depth * columns, bytes_accessed=4 * depth * columns, transcendentals=0
        ),
    )(cycle_amps, panel)


DEPTH = 16
GROUP = 4
SLOTS = 6
PART = 2


def ladder_kernel(own_hbm, other, amp_hbm, fitted_hbm, near_ref, keep_ref, send_ref,
                  own, amp, amp_high, amp_low, rows_ref, left, fitted_in, total, sems, fitted_sems):
    pairs, fit_count, virtuals = amp_hbm.shape
    aux_half, a_count = own.shape[:2]
    steps = aux_half // DEPTH
    core, exc, col = lax.axis_index("grp") % 2, lax.axis_index("exc"), lax.axis_index("col")
    first = core * aux_half
    m = 2 * a_count * pairs

    def fetch(step, slot):
        source = fitted_hbm.at[pl.ds(first + step * DEPTH, DEPTH)]
        return pltpu.make_async_copy(source, fitted_in.at[slot], fitted_sems.at[slot])

    small = [
        pltpu.make_async_copy(amp_hbm, amp, sems.at[0]),
        pltpu.make_async_copy(own_hbm.at[pl.ds(first, aux_half)], own, sems.at[1]),
    ]
    for copy in small:
        copy.start()
    fetch(0, 0).start()
    total[...] = jnp.zeros_like(total)
    small[0].wait()
    fetch(1, 1).start()
    for pair in range(pairs):
        high, low = split(amp[pair])
        amp_high[pl.ds(pair * fit_count, fit_count), :] = high
        amp_low[pl.ds(pair * fit_count, fit_count), :] = low
    small[1].wait()
    for step in range(2, SLOTS):
        fetch(step, step).start()

    def first_product(group):
        count = DEPTH * GROUP
        for p in range(count):
            rows_ref[pl.ds(2 * a_count * p, a_count), :] = own[group * count + p]
            rows_ref[pl.ds(2 * a_count * p + a_count, a_count), :] = other[first + group * count + p]
        high, low = split(rows_ref[...])
        stacked = jnp.concatenate([high, low], axis=0)
        n_rows = high.shape[0]
        upper = lax.broadcasted_iota(jnp.int32, (n_rows // 8, 8, LANES), 1) < 4

        for quad in range(pairs // 4):
            lanes = pl.ds(quad * 4 * fit_count, 4 * fit_count)
            both = dot_t(stacked, amp_high[lanes, :])
            product = both[:n_rows] + both[n_rows:] + dot_t(high, amp_low[lanes, :])
            for odd in range(2):
                tiles = []
                for duo in range(2):
                    one = product[:, (2 * duo) * LANES : (2 * duo + 1) * LANES].reshape(n_rows // 8, 8, LANES)
                    two = product[:, (2 * duo + 1) * LANES : (2 * duo + 2) * LANES].reshape(n_rows // 8, 8, LANES)
                    if odd:
                        tiles.append(jnp.where(upper, pltpu.roll(one, 4, 1), two))
                    else:
                        tiles.append(jnp.where(upper, one, pltpu.roll(two, 4, 1)))
                tile_high, tile_low = split(jnp.concatenate(tiles, axis=1))
                for index in range(n_rows // 8):
                    slot, place_in = divmod(2 * index + odd, DEPTH)
                    left[slot, pl.ds(16 * quad, 16), pl.ds(place_in * LANES, LANES)] = tile_high[index]
                    left[slot, pl.ds(m + 16 * quad, 16), pl.ds(place_in * LANES, LANES)] = tile_low[index]

    @pl.loop(0, steps // GROUP)
    def _(group):
        first_product(group)
        for near in range(GROUP):
            step = group * GROUP + near
            slot = lax.rem(step, SLOTS)
            fetch(step, slot).wait()
            for piece in range(DEPTH // PART):
                fitted = fitted_in[slot, pl.ds(piece * PART, PART)].reshape(PART * fit_count, virtuals)
                fitted_high, fitted_low = split(fitted)
                lanes = pl.ds(piece * PART * LANES, PART * LANES)
                both = dot(left[near, :, lanes], fitted_high)
                total[...] += both[:m] + both[m:] + dot(left[near, pl.ds(0, m), lanes], fitted_low)

            @pl.when(step + SLOTS < steps)
            def _():
                fetch(step + SLOTS, slot).start()

    for target, out in ((0, keep_ref), (1, send_ref)):
        for far in range(2):
            for away in range(NJ // 2):
                for i in range(NI):
                    for j in range(2):
                        pair = i * NJ + (col ^ away) * 2 + j
                        row = pair * 2 * a_count + target * a_count + (exc ^ far)
                        columns = pl.ds(j * virtuals, virtuals)
                        value = total[pl.ds(row, 1), :]
                        if away == 0:
                            value += near_ref[target * 2 + far, pl.ds(i, 1), columns]
                        out[far, pl.ds(away * NI + i, 1), columns] = value


def ladder_slots(own, other, pair_amps, fitted_factor, near):
    pairs, fit_count, virtuals = pair_amps.shape
    aux_count, a_count = own.shape[:2]
    m = 2 * a_count * pairs
    out = jax.ShapeDtypeStruct((2, NJ, 2 * virtuals), jnp.float32)
    half = (aux_count // 2, a_count, virtuals)
    return pl.pallas_call(
        ladder_kernel,
        out_shape=(out, out),
        in_specs=[
            pl.BlockSpec(memory_space=pltpu.HBM),
            pl.BlockSpec(memory_space=pltpu.VMEM),
            pl.BlockSpec(memory_space=pltpu.HBM),
            pl.BlockSpec(memory_space=pltpu.HBM),
            pl.BlockSpec(memory_space=pltpu.VMEM),
        ],
        out_specs=(pl.BlockSpec(memory_space=pltpu.VMEM),) * 2,
        scratch_shapes=[
            pltpu.VMEM(half, jnp.float32),
            pltpu.VMEM(pair_amps.shape, jnp.float32),
            pltpu.VMEM((pairs * fit_count, virtuals), jnp.bfloat16),
            pltpu.VMEM((pairs * fit_count, virtuals), jnp.bfloat16),
            pltpu.VMEM((DEPTH * GROUP * 2 * a_count, virtuals), jnp.float32),
            pltpu.VMEM((GROUP, 2 * m, DEPTH * LANES), jnp.bfloat16),
            pltpu.VMEM((SLOTS, DEPTH, fit_count, virtuals), jnp.float32),
            pltpu.VMEM((m, virtuals), jnp.float32),
            pltpu.SemaphoreType.DMA((2,)),
            pltpu.SemaphoreType.DMA((SLOTS,)),
        ],
        compiler_params=pltpu.CompilerParams(vmem_limit_bytes=VMEM_BYTES),
        cost_estimate=pl.CostEstimate(
            flops=6 * aux_count * a_count * pairs * fit_count * virtuals * 2,
            bytes_accessed=2 * aux_count * fit_count * virtuals, transcendentals=0
        ),
    )(own, other, pair_amps, fitted_factor, near)


def swap(x, axis, size, bit):
    return lax.ppermute(x, axis, [(n, n ^ bit) for n in range(size)])


def fast(grp_count, exc_count, col_count, window_factor, fitted_factor, pair_amps, cycle_amps, panel):
    other = swap(window_factor, "grp", grp_count, 1)
    near, far, across = cycle_slots(cycle_amps, panel)
    one, two = swap(far, "grp", grp_count, 2), swap(across, "grp", grp_count, 3)
    keep, send = ladder_slots(window_factor, other, pair_amps, fitted_factor, near)
    keep, send, one, two = lax.optimization_barrier((keep, send, one, two))
    total = (keep + swap(send, "grp", grp_count, 1)).at[:, :NI].add(one + two)
    total = total[0] + swap(total[1], "exc", exc_count, 1)
    bit = col_count // 2
    while bit:
        total = total[: bit * NI] + swap(total[bit * NI :], "col", col_count, bit)
        bit //= 2
    return total


def solution(mesh):
    placed = (
        P("exc", "grp", None),
        P("exc", "col", None),
        P(None, "col", None),
        P(None, ("grp", "exc")),
        P(("grp", "exc"), "col"),
    )
    grp_count, exc_count, col_count = (mesh.shape[name] for name in ("grp", "exc", "col"))

    def shards(window_factor, fitted_factor, pair_amps, cycle_amps, panel):
        aux_count, a_count, virtuals = window_factor.shape
        fits = (
            grp_count == 4
            and exc_count == 2
            and a_count == 2
            and 2 * col_count == NJ
            and fitted_factor.shape[1] == LANES
            and virtuals % LANES == 0
            and aux_count % (2 * DEPTH * GROUP) == 0
            and cycle_amps.shape[1] % STRIP == 0
        )
        body = functools.partial(fast, grp_count, exc_count, col_count) if fits else plain
        return body(window_factor, fitted_factor, pair_amps, cycle_amps, panel)

    return jax.shard_map(
        shards, mesh=mesh, in_specs=placed, out_specs=P(("grp", "exc"), "col"), check_vma=False
    )
```

```python
import functools

import jax
import jax.numpy as jnp
from jax import lax
from jax.experimental import pallas as pl
from jax.experimental.pallas import tpu as pltpu
from jax.sharding import PartitionSpec as P

NI = 2
NJ = 8
VMEM_BYTES = 38 * 1024 * 1024
LANES = 128


def split(x):
    high = x.astype(jnp.bfloat16)
    low = (x - high.astype(jnp.float32)).astype(jnp.bfloat16)
    return high, low


def dot(x, y):
    return jnp.dot(x, y, preferred_element_type=jnp.float32)


def dot_t(x, y):
    return lax.dot_general(x, y, (((1,), (1,)), ((), ())), preferred_element_type=jnp.float32)


def plain(window_factor, fitted_factor, pair_amps, cycle_amps, panel):
    precise = lax.Precision.HIGHEST
    aux_count, virt_count, virtuals = window_factor.shape
    fit_count = fitted_factor.shape[1]
    amplitude = pair_amps.reshape(NI, NJ, fit_count, virtuals)
    inner = jnp.einsum("pac,ijdc->aijpd", window_factor, amplitude, precision=precise)
    inner_rows = inner.reshape(virt_count * NI * NJ, aux_count * fit_count)
    fitted_rows = fitted_factor.reshape(aux_count * fit_count, virtuals)
    ladder_terms = jnp.dot(inner_rows, fitted_rows, precision=precise, preferred_element_type=jnp.float32)
    ladder_terms = ladder_terms.reshape(virt_count * NI, NJ * virtuals)
    cycle_part = jnp.dot(cycle_amps, panel, precision=precise, preferred_element_type=jnp.float32)
    partial_value = lax.psum_scatter(ladder_terms, "col", scatter_dimension=1, tiled=True)
    ladder = lax.psum_scatter(partial_value, "exc", scatter_dimension=0, tiled=True)
    cycle = lax.psum_scatter(cycle_part, ("grp", "exc"), scatter_dimension=0, tiled=True)
    return ladder + cycle


STRIP = 512
STRIPS = 3


def cycle_kernel(amps_hbm, panel_ref, near_ref, far_ref, across_ref, amps_ref, strips, total, sems, amps_sem):
    rows, depth = amps_ref.shape
    count = depth // STRIP
    me = lax.axis_index("grp") * lax.axis_size("exc") + lax.axis_index("exc")
    amps_copy = pltpu.make_async_copy(amps_hbm, amps_ref, amps_sem)
    amps_copy.start()

    def fetch(n):
        return pltpu.make_async_copy(panel_ref.at[pl.ds(n * STRIP, STRIP)], strips.at[n], sems.at[n])

    for n in range(min(STRIPS, count)):
        fetch(n).start()
    total[...] = jnp.zeros_like(total)
    amps_copy.wait()
    for n in range(count):
        fetch(n).wait()
        if n + STRIPS < count:
            fetch(n + STRIPS).start()
        high, low = split(amps_ref[:, n * STRIP : (n + 1) * STRIP])
        panel_high, panel_low = split(strips[n])
        both = dot(jnp.concatenate([high, low], axis=0), panel_high)
        total[...] += both[:rows] + both[rows:] + dot(high, panel_low)
    exc_count = lax.axis_size("exc")
    outs = [(near_ref, n) for n in range(2 * exc_count)]
    outs += [(ref, n) for ref in (far_ref, across_ref) for n in range(exc_count)]
    for slot, (out, n) in enumerate(outs):
        row = (me ^ slot) * NI
        for i in range(NI):
            out[n, pl.ds(i, 1), :] = total[pl.ds(row + i, 1), :]


def cycle_slots(cycle_amps, panel):
    rows, depth = cycle_amps.shape
    columns = panel.shape[1]
    near = jax.ShapeDtypeStruct((rows // NI // 2, NI, columns), jnp.float32)
    far = jax.ShapeDtypeStruct((rows // NI // 4, NI, columns), jnp.float32)
    return pl.pallas_call(
        cycle_kernel,
        out_shape=(near, far, far),
        in_specs=[pl.BlockSpec(memory_space=pltpu.HBM)] * 2,
        out_specs=(pl.BlockSpec(memory_space=pltpu.VMEM),) * 3,
        scratch_shapes=[
            pltpu.VMEM((rows, depth), jnp.float32),
            pltpu.VMEM((depth // STRIP, STRIP, columns), jnp.float32),
            pltpu.VMEM((rows, columns), jnp.float32),
            pltpu.SemaphoreType.DMA((depth // STRIP,)),
            pltpu.SemaphoreType.DMA,
        ],
        compiler_params=pltpu.CompilerParams(vmem_limit_bytes=VMEM_BYTES),
        cost_estimate=pl.CostEstimate(
            flops=6 * rows * depth * columns, bytes_accessed=4 * depth * columns, transcendentals=0
        ),
    )(cycle_amps, panel)


DEPTH = 16
GROUP = 4
SLOTS = 6
PART = 2


def ladder_kernel(own, other, amp, fitted_hbm, near_ref, keep_ref, send_ref,
                  amp_high, amp_low, rows_ref, left, fitted_in, total, fitted_sems):
    pairs, fit_count, virtuals = amp.shape
    aux_half, a_count = own.shape[0] // 2, own.shape[1]
    steps = aux_half // DEPTH
    core, exc, col = lax.axis_index("grp") % 2, lax.axis_index("exc"), lax.axis_index("col")
    first = core * aux_half
    m = 2 * a_count * pairs

    def fetch(step, slot):
        source = fitted_hbm.at[pl.ds(first + step * DEPTH, DEPTH)]
        return pltpu.make_async_copy(source, fitted_in.at[slot], fitted_sems.at[slot])

    fetch(0, 0).start()
    total[...] = jnp.zeros_like(total)
    fetch(1, 1).start()
    for pair in range(pairs):
        high, low = split(amp[pair])
        amp_high[pl.ds(pair * fit_count, fit_count), :] = high
        amp_low[pl.ds(pair * fit_count, fit_count), :] = low
    for step in range(2, SLOTS):
        fetch(step, step).start()

    def first_product(group):
        count = DEPTH * GROUP
        for p in range(count):
            rows_ref[pl.ds(2 * a_count * p, a_count), :] = own[first + group * count + p]
            rows_ref[pl.ds(2 * a_count * p + a_count, a_count), :] = other[first + group * count + p]
        high, low = split(rows_ref[...])
        stacked = jnp.concatenate([high, low], axis=0)
        n_rows = high.shape[0]
        upper = lax.broadcasted_iota(jnp.int32, (n_rows // 8, 8, LANES), 1) < 4

        for quad in range(pairs // 4):
            lanes = pl.ds(quad * 4 * fit_count, 4 * fit_count)
            both = dot_t(stacked, amp_high[lanes, :])
            product = both[:n_rows] + both[n_rows:] + dot_t(high, amp_low[lanes, :])
            for odd in range(2):
                tiles = []
                for duo in range(2):
                    one = product[:, (2 * duo) * LANES : (2 * duo + 1) * LANES].reshape(n_rows // 8, 8, LANES)
                    two = product[:, (2 * duo + 1) * LANES : (2 * duo + 2) * LANES].reshape(n_rows // 8, 8, LANES)
                    if odd:
                        tiles.append(jnp.where(upper, pltpu.roll(one, 4, 1), two))
                    else:
                        tiles.append(jnp.where(upper, one, pltpu.roll(two, 4, 1)))
                tile_high, tile_low = split(jnp.concatenate(tiles, axis=1))
                for index in range(n_rows // 8):
                    slot, place_in = divmod(2 * index + odd, DEPTH)
                    left[slot, pl.ds(16 * quad, 16), pl.ds(place_in * LANES, LANES)] = tile_high[index]
                    left[slot, pl.ds(m + 16 * quad, 16), pl.ds(place_in * LANES, LANES)] = tile_low[index]

    @pl.loop(0, steps // GROUP)
    def _(group):
        first_product(group)
        for near in range(GROUP):
            step = group * GROUP + near
            slot = lax.rem(step, SLOTS)
            fetch(step, slot).wait()
            for piece in range(DEPTH // PART):
                fitted = fitted_in[slot, pl.ds(piece * PART, PART)].reshape(PART * fit_count, virtuals)
                fitted_high, fitted_low = split(fitted)
                lanes = pl.ds(piece * PART * LANES, PART * LANES)
                both = dot(left[near, :, lanes], fitted_high)
                total[...] += both[:m] + both[m:] + dot(left[near, pl.ds(0, m), lanes], fitted_low)

            @pl.when(step + SLOTS < steps)
            def _():
                fetch(step + SLOTS, slot).start()

    for target, out in ((0, keep_ref), (1, send_ref)):
        for far in range(2):
            for away in range(NJ // 2):
                for i in range(NI):
                    for j in range(2):
                        pair = i * NJ + (col ^ away) * 2 + j
                        row = pair * 2 * a_count + target * a_count + (exc ^ far)
                        columns = pl.ds(j * virtuals, virtuals)
                        value = total[pl.ds(row, 1), :]
                        if away == 0:
                            value += near_ref[target * 2 + far, pl.ds(i, 1), columns]
                        out[far, pl.ds(away * NI + i, 1), columns] = value


def ladder_slots(own, other, pair_amps, fitted_factor, near):
    pairs, fit_count, virtuals = pair_amps.shape
    aux_count, a_count = own.shape[:2]
    m = 2 * a_count * pairs
    out = jax.ShapeDtypeStruct((2, NJ, 2 * virtuals), jnp.float32)
    return pl.pallas_call(
        ladder_kernel,
        out_shape=(out, out),
        in_specs=[
            pl.BlockSpec(memory_space=pltpu.VMEM),
            pl.BlockSpec(memory_space=pltpu.VMEM),
            pl.BlockSpec(memory_space=pltpu.VMEM),
            pl.BlockSpec(memory_space=pltpu.HBM),
            pl.BlockSpec(memory_space=pltpu.VMEM),
        ],
        out_specs=(pl.BlockSpec(memory_space=pltpu.VMEM),) * 2,
        scratch_shapes=[
            pltpu.VMEM((pairs * fit_count, virtuals), jnp.bfloat16),
            pltpu.VMEM((pairs * fit_count, virtuals), jnp.bfloat16),
            pltpu.VMEM((DEPTH * GROUP * 2 * a_count, virtuals), jnp.float32),
            pltpu.VMEM((GROUP, 2 * m, DEPTH * LANES), jnp.bfloat16),
            pltpu.VMEM((SLOTS, DEPTH, fit_count, virtuals), jnp.float32),
            pltpu.VMEM((m, virtuals), jnp.float32),
            pltpu.SemaphoreType.DMA((SLOTS,)),
        ],
        compiler_params=pltpu.CompilerParams(vmem_limit_bytes=VMEM_BYTES),
        cost_estimate=pl.CostEstimate(
            flops=6 * aux_count * a_count * pairs * fit_count * virtuals * 2,
            bytes_accessed=2 * aux_count * fit_count * virtuals, transcendentals=0
        ),
    )(own, other, pair_amps, fitted_factor, near)


def swap(x, axis, size, bit):
    return lax.ppermute(x, axis, [(n, n ^ bit) for n in range(size)])


def fast(grp_count, exc_count, col_count, window_factor, fitted_factor, pair_amps, cycle_amps, panel):
    other = swap(window_factor, "grp", grp_count, 1)
    near, far, across = cycle_slots(cycle_amps, panel)
    one, two = swap(far, "grp", grp_count, 2), swap(across, "grp", grp_count, 3)
    keep, send = ladder_slots(window_factor, other, pair_amps, fitted_factor, near)
    keep, send, one, two = lax.optimization_barrier((keep, send, one, two))
    total = (keep + swap(send, "grp", grp_count, 1)).at[:, :NI].add(one + two)
    total = total[0] + swap(total[1], "exc", exc_count, 1)
    bit = col_count // 2
    while bit:
        total = total[: bit * NI] + swap(total[bit * NI :], "col", col_count, bit)
        bit //= 2
    return total


def solution(mesh):
    placed = (
        P("exc", "grp", None),
        P("exc", "col", None),
        P(None, "col", None),
        P(None, ("grp", "exc")),
        P(("grp", "exc"), "col"),
    )
    grp_count, exc_count, col_count = (mesh.shape[name] for name in ("grp", "exc", "col"))

    def shards(window_factor, fitted_factor, pair_amps, cycle_amps, panel):
        aux_count, a_count, virtuals = window_factor.shape
        fits = (
            grp_count == 4
            and exc_count == 2
            and a_count == 2
            and 2 * col_count == NJ
            and fitted_factor.shape[1] == LANES
            and virtuals % LANES == 0
            and aux_count % (2 * DEPTH * GROUP) == 0
            and cycle_amps.shape[1] % STRIP == 0
        )
        body = functools.partial(fast, grp_count, exc_count, col_count) if fits else plain
        return body(window_factor, fitted_factor, pair_amps, cycle_amps, panel)

    return jax.shard_map(
        shards, mesh=mesh, in_specs=placed, out_specs=P(("grp", "exc"), "col"), check_vma=False
    )
```

```python
import functools

import jax
import jax.numpy as jnp
from jax import lax
from jax.experimental import pallas as pl
from jax.experimental.pallas import tpu as pltpu
from jax.sharding import PartitionSpec as P

NI = 2
NJ = 8
VMEM_BYTES = 38 * 1024 * 1024
LANES = 128


def split(x):
    high = x.astype(jnp.bfloat16)
    low = (x - high.astype(jnp.float32)).astype(jnp.bfloat16)
    return high, low


def dot(x, y):
    return jnp.dot(x, y, preferred_element_type=jnp.float32)


def dot_t(x, y):
    return lax.dot_general(x, y, (((1,), (1,)), ((), ())), preferred_element_type=jnp.float32)


def plain(window_factor, fitted_factor, pair_amps, cycle_amps, panel):
    precise = lax.Precision.HIGHEST
    aux_count, virt_count, virtuals = window_factor.shape
    fit_count = fitted_factor.shape[1]
    amplitude = pair_amps.reshape(NI, NJ, fit_count, virtuals)
    inner = jnp.einsum("pac,ijdc->aijpd", window_factor, amplitude, precision=precise)
    inner_rows = inner.reshape(virt_count * NI * NJ, aux_count * fit_count)
    fitted_rows = fitted_factor.reshape(aux_count * fit_count, virtuals)
    ladder_terms = jnp.dot(inner_rows, fitted_rows, precision=precise, preferred_element_type=jnp.float32)
    ladder_terms = ladder_terms.reshape(virt_count * NI, NJ * virtuals)
    cycle_part = jnp.dot(cycle_amps, panel, precision=precise, preferred_element_type=jnp.float32)
    partial_value = lax.psum_scatter(ladder_terms, "col", scatter_dimension=1, tiled=True)
    ladder = lax.psum_scatter(partial_value, "exc", scatter_dimension=0, tiled=True)
    cycle = lax.psum_scatter(cycle_part, ("grp", "exc"), scatter_dimension=0, tiled=True)
    return ladder + cycle


STRIP = 512
STRIPS = 3


def cycle_kernel(amps_hbm, panel_ref, near_ref, far_ref, across_ref, amps_ref, strips, total, sems, amps_sem):
    rows, depth = amps_ref.shape
    count = depth // STRIP
    me = lax.axis_index("grp") * lax.axis_size("exc") + lax.axis_index("exc")
    amps_copy = pltpu.make_async_copy(amps_hbm, amps_ref, amps_sem)
    amps_copy.start()

    def fetch(n):
        return pltpu.make_async_copy(panel_ref.at[pl.ds(n * STRIP, STRIP)], strips.at[n], sems.at[n])

    for n in range(min(STRIPS, count)):
        fetch(n).start()
    total[...] = jnp.zeros_like(total)
    amps_copy.wait()
    for n in range(count):
        fetch(n).wait()
        if n + STRIPS < count:
            fetch(n + STRIPS).start()
        high, low = split(amps_ref[:, n * STRIP : (n + 1) * STRIP])
        panel_high, panel_low = split(strips[n])
        both = dot(jnp.concatenate([high, low], axis=0), panel_high)
        total[...] += both[:rows] + both[rows:] + dot(high, panel_low)
    exc_count = lax.axis_size("exc")
    outs = [(near_ref, n) for n in range(2 * exc_count)]
    outs += [(ref, n) for ref in (far_ref, across_ref) for n in range(exc_count)]
    for slot, (out, n) in enumerate(outs):
        row = (me ^ slot) * NI
        for i in range(NI):
            out[n, pl.ds(i, 1), :] = total[pl.ds(row + i, 1), :]


def cycle_slots(cycle_amps, panel):
    rows, depth = cycle_amps.shape
    columns = panel.shape[1]
    near = jax.ShapeDtypeStruct((rows // NI // 2, NI, columns), jnp.float32)
    far = jax.ShapeDtypeStruct((rows // NI // 4, NI, columns), jnp.float32)
    return pl.pallas_call(
        cycle_kernel,
        out_shape=(near, far, far),
        in_specs=[pl.BlockSpec(memory_space=pltpu.HBM)] * 2,
        out_specs=(pl.BlockSpec(memory_space=pltpu.VMEM),) * 3,
        scratch_shapes=[
            pltpu.VMEM((rows, depth), jnp.float32),
            pltpu.VMEM((depth // STRIP, STRIP, columns), jnp.float32),
            pltpu.VMEM((rows, columns), jnp.float32),
            pltpu.SemaphoreType.DMA((depth // STRIP,)),
            pltpu.SemaphoreType.DMA,
        ],
        compiler_params=pltpu.CompilerParams(vmem_limit_bytes=VMEM_BYTES),
        cost_estimate=pl.CostEstimate(
            flops=6 * rows * depth * columns, bytes_accessed=4 * depth * columns, transcendentals=0
        ),
    )(cycle_amps, panel)


DEPTH = 16
GROUP = 4
SLOTS = 6
PART = 2


def ladder_kernel(own, other, amp, fitted_hbm, near_ref, keep_ref, send_ref,
                  amp_high, amp_low, rows_ref, left, fitted_in, total, fitted_sems):
    pairs, fit_count, virtuals = amp.shape
    aux_half, a_count = own.shape[0] // 2, own.shape[1]
    steps = aux_half // DEPTH
    core, exc, col = lax.axis_index("grp") % 2, lax.axis_index("exc"), lax.axis_index("col")
    first = core * aux_half
    m = 2 * a_count * pairs

    def fetch(step, slot):
        source = fitted_hbm.at[pl.ds(first + step * DEPTH, DEPTH)]
        return pltpu.make_async_copy(source, fitted_in.at[slot], fitted_sems.at[slot])

    fetch(0, 0).start()
    total[...] = jnp.zeros_like(total)
    fetch(1, 1).start()
    for pair in range(pairs):
        high, low = split(amp[pair])
        amp_high[pl.ds(pair * fit_count, fit_count), :] = high
        amp_low[pl.ds(pair * fit_count, fit_count), :] = low
    for step in range(2, SLOTS):
        fetch(step, step).start()

    def first_product(group):
        count = DEPTH * GROUP
        for p in range(count):
            rows_ref[pl.ds(2 * a_count * p, a_count), :] = own[first + group * count + p]
            rows_ref[pl.ds(2 * a_count * p + a_count, a_count), :] = other[first + group * count + p]
        high, low = split(rows_ref[...])
        stacked = jnp.concatenate([high, low], axis=0)
        n_rows = high.shape[0]
        upper = lax.broadcasted_iota(jnp.int32, (n_rows // 8, 8, LANES), 1) < 4

        for quad in range(pairs // 4):
            lanes = pl.ds(quad * 4 * fit_count, 4 * fit_count)
            both = dot_t(stacked, amp_high[lanes, :])
            product = both[:n_rows] + both[n_rows:] + dot_t(high, amp_low[lanes, :])
            for odd in range(2):
                tiles = []
                for duo in range(2):
                    one = product[:, (2 * duo) * LANES : (2 * duo + 1) * LANES].reshape(n_rows // 8, 8, LANES)
                    two = product[:, (2 * duo + 1) * LANES : (2 * duo + 2) * LANES].reshape(n_rows // 8, 8, LANES)
                    if odd:
                        tiles.append(jnp.where(upper, pltpu.roll(one, 4, 1), two))
                    else:
                        tiles.append(jnp.where(upper, one, pltpu.roll(two, 4, 1)))
                tile_high, tile_low = split(jnp.concatenate(tiles, axis=1))
                for index in range(n_rows // 8):
                    slot, place_in = divmod(2 * index + odd, DEPTH)
                    left[slot, pl.ds(16 * quad, 16), pl.ds(place_in * LANES, LANES)] = tile_high[index]
                    left[slot, pl.ds(m + 16 * quad, 16), pl.ds(place_in * LANES, LANES)] = tile_low[index]

    @pl.loop(0, steps // GROUP)
    def _(group):
        first_product(group)
        for near in range(GROUP):
            step = group * GROUP + near
            slot = lax.rem(step, SLOTS)
            fetch(step, slot).wait()
            for piece in range(DEPTH // PART):
                fitted = fitted_in[slot, pl.ds(piece * PART, PART)].reshape(PART * fit_count, virtuals)
                fitted_high, fitted_low = split(fitted)
                lanes = pl.ds(piece * PART * LANES, PART * LANES)
                both = dot(left[near, :, lanes], fitted_high)
                total[...] += both[:m] + both[m:] + dot(left[near, pl.ds(0, m), lanes], fitted_low)

            @pl.when(step + SLOTS < steps)
            def _():
                fetch(step + SLOTS, slot).start()

    for target, out in ((0, keep_ref), (1, send_ref)):
        for far in range(2):
            for away in range(NJ // 2):
                for i in range(NI):
                    for j in range(2):
                        pair = i * NJ + (col ^ away) * 2 + j
                        row = pair * 2 * a_count + target * a_count + (exc ^ far)
                        columns = pl.ds(j * virtuals, virtuals)
                        value = total[pl.ds(row, 1), :]
                        if away == 0:
                            value += near_ref[target * 2 + far, pl.ds(i, 1), columns]
                        out[far, pl.ds(away * NI + i, 1), columns] = value


def ladder_slots(own, other, pair_amps, fitted_factor, near):
    pairs, fit_count, virtuals = pair_amps.shape
    aux_count, a_count = own.shape[:2]
    m = 2 * a_count * pairs
    out = jax.ShapeDtypeStruct((2, NJ, 2 * virtuals), jnp.float32)
    return pl.pallas_call(
        ladder_kernel,
        out_shape=(out, out),
        in_specs=[
            pl.BlockSpec(memory_space=pltpu.VMEM),
            pl.BlockSpec(memory_space=pltpu.VMEM),
            pl.BlockSpec(memory_space=pltpu.VMEM),
            pl.BlockSpec(memory_space=pltpu.HBM),
            pl.BlockSpec(memory_space=pltpu.VMEM),
        ],
        out_specs=(pl.BlockSpec(memory_space=pltpu.VMEM),) * 2,
        scratch_shapes=[
            pltpu.VMEM((pairs * fit_count, virtuals), jnp.bfloat16),
            pltpu.VMEM((pairs * fit_count, virtuals), jnp.bfloat16),
            pltpu.VMEM((DEPTH * GROUP * 2 * a_count, virtuals), jnp.float32),
            pltpu.VMEM((GROUP, 2 * m, DEPTH * LANES), jnp.bfloat16),
            pltpu.VMEM((SLOTS, DEPTH, fit_count, virtuals), jnp.float32),
            pltpu.VMEM((m, virtuals), jnp.float32),
            pltpu.SemaphoreType.DMA((SLOTS,)),
        ],
        compiler_params=pltpu.CompilerParams(vmem_limit_bytes=VMEM_BYTES),
        cost_estimate=pl.CostEstimate(
            flops=6 * aux_count * a_count * pairs * fit_count * virtuals * 2,
            bytes_accessed=2 * aux_count * fit_count * virtuals, transcendentals=0
        ),
    )(own, other, pair_amps, fitted_factor, near)


def swap(x, axis, size, bit):
    return lax.ppermute(x, axis, [(n, n ^ bit) for n in range(size)])


def fast(grp_count, exc_count, col_count, window_factor, fitted_factor, pair_amps, cycle_amps, panel):
    other = swap(window_factor, "grp", grp_count, 1)
    near, far, across = cycle_slots(cycle_amps, panel)
    keep, send = ladder_slots(window_factor, other, pair_amps, fitted_factor, near)
    keep, send, far, across = lax.optimization_barrier((keep, send, far, across))
    total = keep + swap(send, "grp", grp_count, 1)
    one, two = swap(far, "grp", grp_count, 2), swap(across, "grp", grp_count, 3)
    bit = col_count // 2
    while bit:
        total = total[:, : bit * NI] + swap(total[:, bit * NI :], "col", col_count, bit)
        bit //= 2
    total = total + (one + two)
    total = total[0] + swap(total[1], "exc", exc_count, 1)
    return total


def solution(mesh):
    placed = (
        P("exc", "grp", None),
        P("exc", "col", None),
        P(None, "col", None),
        P(None, ("grp", "exc")),
        P(("grp", "exc"), "col"),
    )
    grp_count, exc_count, col_count = (mesh.shape[name] for name in ("grp", "exc", "col"))

    def shards(window_factor, fitted_factor, pair_amps, cycle_amps, panel):
        aux_count, a_count, virtuals = window_factor.shape
        fits = (
            grp_count == 4
            and exc_count == 2
            and a_count == 2
            and 2 * col_count == NJ
            and fitted_factor.shape[1] == LANES
            and virtuals % LANES == 0
            and aux_count % (2 * DEPTH * GROUP) == 0
            and cycle_amps.shape[1] % STRIP == 0
        )
        body = functools.partial(fast, grp_count, exc_count, col_count) if fits else plain
        return body(window_factor, fitted_factor, pair_amps, cycle_amps, panel)

    return jax.shard_map(
        shards, mesh=mesh, in_specs=placed, out_specs=P(("grp", "exc"), "col"), check_vma=False
    )
```

```python
import functools

import jax
import jax.numpy as jnp
from jax import lax
from jax.experimental import pallas as pl
from jax.experimental.pallas import tpu as pltpu
from jax.sharding import PartitionSpec as P

NI = 2
NJ = 8
VMEM_BYTES = 38 * 1024 * 1024
LANES = 128


def split(x):
    high = x.astype(jnp.bfloat16)
    low = (x - high.astype(jnp.float32)).astype(jnp.bfloat16)
    return high, low


def dot(x, y):
    return jnp.dot(x, y, preferred_element_type=jnp.float32)


def dot_t(x, y):
    return lax.dot_general(x, y, (((1,), (1,)), ((), ())), preferred_element_type=jnp.float32)


def plain(window_factor, fitted_factor, pair_amps, cycle_amps, panel):
    precise = lax.Precision.HIGHEST
    aux_count, virt_count, virtuals = window_factor.shape
    fit_count = fitted_factor.shape[1]
    amplitude = pair_amps.reshape(NI, NJ, fit_count, virtuals)
    inner = jnp.einsum("pac,ijdc->aijpd", window_factor, amplitude, precision=precise)
    inner_rows = inner.reshape(virt_count * NI * NJ, aux_count * fit_count)
    fitted_rows = fitted_factor.reshape(aux_count * fit_count, virtuals)
    ladder_terms = jnp.dot(inner_rows, fitted_rows, precision=precise, preferred_element_type=jnp.float32)
    ladder_terms = ladder_terms.reshape(virt_count * NI, NJ * virtuals)
    cycle_part = jnp.dot(cycle_amps, panel, precision=precise, preferred_element_type=jnp.float32)
    partial_value = lax.psum_scatter(ladder_terms, "col", scatter_dimension=1, tiled=True)
    ladder = lax.psum_scatter(partial_value, "exc", scatter_dimension=0, tiled=True)
    cycle = lax.psum_scatter(cycle_part, ("grp", "exc"), scatter_dimension=0, tiled=True)
    return ladder + cycle


STRIP = 512
STRIPS = 3


def cycle_kernel(amps_hbm, panel_ref, near_ref, far_ref, across_ref, amps_ref, strips, total, sems, amps_sem):
    rows, depth = amps_ref.shape
    count = depth // STRIP
    me = lax.axis_index("grp") * lax.axis_size("exc") + lax.axis_index("exc")
    amps_copy = pltpu.make_async_copy(amps_hbm, amps_ref, amps_sem)
    amps_copy.start()

    def fetch(n):
        return pltpu.make_async_copy(panel_ref.at[pl.ds(n * STRIP, STRIP)], strips.at[n], sems.at[n])

    for n in range(min(STRIPS, count)):
        fetch(n).start()
    total[...] = jnp.zeros_like(total)
    amps_copy.wait()
    for n in range(count):
        fetch(n).wait()
        if n + STRIPS < count:
            fetch(n + STRIPS).start()
        high, low = split(amps_ref[:, n * STRIP : (n + 1) * STRIP])
        panel_high, panel_low = split(strips[n])
        both = dot(jnp.concatenate([high, low], axis=0), panel_high)
        total[...] += both[:rows] + both[rows:] + dot(high, panel_low)
    exc_count = lax.axis_size("exc")
    outs = [(near_ref, n) for n in range(2 * exc_count)]
    outs += [(ref, n) for ref in (far_ref, across_ref) for n in range(exc_count)]
    for slot, (out, n) in enumerate(outs):
        row = (me ^ slot) * NI
        for i in range(NI):
            out[n, pl.ds(i, 1), :] = total[pl.ds(row + i, 1), :]


def cycle_slots(cycle_amps, panel):
    rows, depth = cycle_amps.shape
    columns = panel.shape[1]
    near = jax.ShapeDtypeStruct((rows // NI // 2, NI, columns), jnp.float32)
    far = jax.ShapeDtypeStruct((rows // NI // 4, NI, columns), jnp.float32)
    return pl.pallas_call(
        cycle_kernel,
        out_shape=(near, far, far),
        in_specs=[pl.BlockSpec(memory_space=pltpu.HBM)] * 2,
        out_specs=(pl.BlockSpec(memory_space=pltpu.VMEM),) * 3,
        scratch_shapes=[
            pltpu.VMEM((rows, depth), jnp.float32),
            pltpu.VMEM((depth // STRIP, STRIP, columns), jnp.float32),
            pltpu.VMEM((rows, columns), jnp.float32),
            pltpu.SemaphoreType.DMA((depth // STRIP,)),
            pltpu.SemaphoreType.DMA,
        ],
        compiler_params=pltpu.CompilerParams(vmem_limit_bytes=VMEM_BYTES),
        cost_estimate=pl.CostEstimate(
            flops=6 * rows * depth * columns, bytes_accessed=4 * depth * columns, transcendentals=0
        ),
    )(cycle_amps, panel)


DEPTH = 16
GROUP = 4
SLOTS = 6
PART = 2


def ladder_kernel(own, other, amp, fitted_hbm, near_ref, keep_ref, send_ref,
                  amp_high, amp_low, rows_ref, left, fitted_in, total, fitted_sems):
    pairs, fit_count, virtuals = amp.shape
    aux_half, a_count = own.shape[0] // 2, own.shape[1]
    steps = aux_half // DEPTH
    core, exc, col = lax.axis_index("grp") % 2, lax.axis_index("exc"), lax.axis_index("col")
    first = core * aux_half
    m = 2 * a_count * pairs

    def fetch(step, slot):
        source = fitted_hbm.at[pl.ds(first + step * DEPTH, DEPTH)]
        return pltpu.make_async_copy(source, fitted_in.at[slot], fitted_sems.at[slot])

    fetch(0, 0).start()
    total[...] = jnp.zeros_like(total)
    fetch(1, 1).start()
    for pair in range(pairs):
        high, low = split(amp[pair])
        amp_high[pl.ds(pair * fit_count, fit_count), :] = high
        amp_low[pl.ds(pair * fit_count, fit_count), :] = low
    for step in range(2, SLOTS):
        fetch(step, step).start()

    def first_product(group):
        count = DEPTH * GROUP
        for p in range(count):
            rows_ref[pl.ds(2 * a_count * p, a_count), :] = own[first + group * count + p]
            rows_ref[pl.ds(2 * a_count * p + a_count, a_count), :] = other[first + group * count + p]
        high, low = split(rows_ref[...])
        stacked = jnp.concatenate([high, low], axis=0)
        n_rows = high.shape[0]
        upper = lax.broadcasted_iota(jnp.int32, (n_rows // 8, 8, LANES), 1) < 4

        for quad in range(pairs // 4):
            lanes = pl.ds(quad * 4 * fit_count, 4 * fit_count)
            both = dot_t(stacked, amp_high[lanes, :])
            product = both[:n_rows] + both[n_rows:] + dot_t(high, amp_low[lanes, :])
            for odd in range(2):
                tiles = []
                for duo in range(2):
                    one = product[:, (2 * duo) * LANES : (2 * duo + 1) * LANES].reshape(n_rows // 8, 8, LANES)
                    two = product[:, (2 * duo + 1) * LANES : (2 * duo + 2) * LANES].reshape(n_rows // 8, 8, LANES)
                    if odd:
                        tiles.append(jnp.where(upper, pltpu.roll(one, 4, 1), two))
                    else:
                        tiles.append(jnp.where(upper, one, pltpu.roll(two, 4, 1)))
                tile_high, tile_low = split(jnp.concatenate(tiles, axis=1))
                for index in range(n_rows // 8):
                    slot, place_in = divmod(2 * index + odd, DEPTH)
                    left[slot, pl.ds(16 * quad, 16), pl.ds(place_in * LANES, LANES)] = tile_high[index]
                    left[slot, pl.ds(m + 16 * quad, 16), pl.ds(place_in * LANES, LANES)] = tile_low[index]

    @pl.loop(0, steps // GROUP)
    def _(group):
        first_product(group)
        for near in range(GROUP):
            step = group * GROUP + near
            slot = lax.rem(step, SLOTS)
            fetch(step, slot).wait()
            for piece in range(DEPTH // PART):
                fitted = fitted_in[slot, pl.ds(piece * PART, PART)].reshape(PART * fit_count, virtuals)
                fitted_high, fitted_low = split(fitted)
                lanes = pl.ds(piece * PART * LANES, PART * LANES)
                both = dot(left[near, :, lanes], fitted_high)
                total[...] += both[:m] + both[m:] + dot(left[near, pl.ds(0, m), lanes], fitted_low)

            @pl.when(step + SLOTS < steps)
            def _():
                fetch(step + SLOTS, slot).start()

    order = [0]
    while len(order) < NJ // 2:
        order = [2 * n for n in order] + [2 * n + 1 for n in order]
    for target, out in ((0, keep_ref), (1, send_ref)):
        for far in range(2):
            for place_in, away in enumerate(order):
                for i in range(NI):
                    for j in range(2):
                        pair = i * NJ + (col ^ away) * 2 + j
                        row = pair * 2 * a_count + target * a_count + (exc ^ far)
                        columns = pl.ds(j * virtuals, virtuals)
                        value = total[pl.ds(row, 1), :]
                        if away == 0:
                            value += near_ref[target * 2 + far, pl.ds(i, 1), columns]
                        out[far, pl.ds(place_in * NI + i, 1), columns] = value


def ladder_slots(own, other, pair_amps, fitted_factor, near):
    pairs, fit_count, virtuals = pair_amps.shape
    aux_count, a_count = own.shape[:2]
    m = 2 * a_count * pairs
    out = jax.ShapeDtypeStruct((2, NJ, 2 * virtuals), jnp.float32)
    return pl.pallas_call(
        ladder_kernel,
        out_shape=(out, out),
        in_specs=[
            pl.BlockSpec(memory_space=pltpu.VMEM),
            pl.BlockSpec(memory_space=pltpu.VMEM),
            pl.BlockSpec(memory_space=pltpu.VMEM),
            pl.BlockSpec(memory_space=pltpu.HBM),
            pl.BlockSpec(memory_space=pltpu.VMEM),
        ],
        out_specs=(pl.BlockSpec(memory_space=pltpu.VMEM),) * 2,
        scratch_shapes=[
            pltpu.VMEM((pairs * fit_count, virtuals), jnp.bfloat16),
            pltpu.VMEM((pairs * fit_count, virtuals), jnp.bfloat16),
            pltpu.VMEM((DEPTH * GROUP * 2 * a_count, virtuals), jnp.float32),
            pltpu.VMEM((GROUP, 2 * m, DEPTH * LANES), jnp.bfloat16),
            pltpu.VMEM((SLOTS, DEPTH, fit_count, virtuals), jnp.float32),
            pltpu.VMEM((m, virtuals), jnp.float32),
            pltpu.SemaphoreType.DMA((SLOTS,)),
        ],
        compiler_params=pltpu.CompilerParams(vmem_limit_bytes=VMEM_BYTES),
        cost_estimate=pl.CostEstimate(
            flops=6 * aux_count * a_count * pairs * fit_count * virtuals * 2,
            bytes_accessed=2 * aux_count * fit_count * virtuals, transcendentals=0
        ),
    )(own, other, pair_amps, fitted_factor, near)


def swap(x, axis, size, bit):
    return lax.ppermute(x, axis, [(n, n ^ bit) for n in range(size)])


def fast(grp_count, exc_count, col_count, window_factor, fitted_factor, pair_amps, cycle_amps, panel):
    other = swap(window_factor, "grp", grp_count, 1)
    near, far, across = cycle_slots(cycle_amps, panel)
    keep, send = ladder_slots(window_factor, other, pair_amps, fitted_factor, near)
    keep, send, far, across = lax.optimization_barrier((keep, send, far, across))
    total = keep + swap(send, "grp", grp_count, 1)
    one, two = swap(far, "grp", grp_count, 2), swap(across, "grp", grp_count, 3)
    bit = 1
    while bit < col_count:
        count = total.shape[1] // 2
        total = total[:, :count] + swap(total[:, count:], "col", col_count, bit)
        bit *= 2
    total = total + (one + two)
    total = total[0] + swap(total[1], "exc", exc_count, 1)
    return total


def solution(mesh):
    placed = (
        P("exc", "grp", None),
        P("exc", "col", None),
        P(None, "col", None),
        P(None, ("grp", "exc")),
        P(("grp", "exc"), "col"),
    )
    grp_count, exc_count, col_count = (mesh.shape[name] for name in ("grp", "exc", "col"))

    def shards(window_factor, fitted_factor, pair_amps, cycle_amps, panel):
        aux_count, a_count, virtuals = window_factor.shape
        fits = (
            grp_count == 4
            and exc_count == 2
            and a_count == 2
            and 2 * col_count == NJ
            and fitted_factor.shape[1] == LANES
            and virtuals % LANES == 0
            and aux_count % (2 * DEPTH * GROUP) == 0
            and cycle_amps.shape[1] % STRIP == 0
        )
        body = functools.partial(fast, grp_count, exc_count, col_count) if fits else plain
        return body(window_factor, fitted_factor, pair_amps, cycle_amps, panel)

    return jax.shard_map(
        shards, mesh=mesh, in_specs=placed, out_specs=P(("grp", "exc"), "col"), check_vma=False
    )
```
